32 devices in a mesh: groups: 2 (over y), tensor: 8 (over z, x), pool: 2 (over core).
Axes of the slice: x: 2, y: 2, z: 4, core: 2. Of those that a mesh axis runs over, the one named last changes fastest.
Arguments:
- hidden: bfloat16 [2048, 8192], P(('groups', 'tensor')), parts along dimension 0, may hold values from -700 to 700
- norm_gain: bfloat16 [8192], replicated, may hold values from 0.25 to 1.75
- kv_weight: bfloat16 [8192, 1024], P('tensor', 'pool'), may hold values from -0.0625 to 0.0625
- down_panels: bfloat16 [256, 2, 4096, 64], P('groups', 'pool', 'tensor'), parts along dimension 0, may hold values from -0.0625 to 0.0625
- up_panels: bfloat16 [256, 2, 32768], P('groups', 'pool', 'tensor'), parts along dimension 0, may hold values from -0.75 to 0.75
- seg_adapter: int32 [16], P('groups'), parts along dimension 0, may hold values from 0 to 127
- slot_of: int32 [256], P('groups'), parts along dimension 0, may hold values from 0 to 127, each once
Outputs:
- key_value: bfloat16 [2048, 1024], P(('groups', 'tensor'), 'pool'), parts along dimension 0
The draws below stay inside these ranges and needn't reach their ends.
There are 2 independent parts, one for each index of `groups`. The reference program is written for one: setup_inputs(seed, part) draws one part's arguments, and reference() takes and returns one part's arrays. A program takes and returns all parts, laid end to end along the dimension named above; an argument that names none is the same for every part. Nothing has to cross between parts.
Inputs may be any that keep to these rules, and one draw needn't show every extreme that they name: `seg_adapter`: adapter of each segment of 128 tokens, in token order. `slot_of`: every adapter has one slot and every slot one adapter.
All inputs are finite; a program needn't handle non-finite values.
Results may differ from the reference program's by a relative error of at most 0.0054.
Values may be sent and summed in bfloat16 or wider, within the bound.
No kernel may reach another device: no remote copies, remote signals or barrier semaphores. Data moves between devices by JAX's collectives and lax.ppermute only.
A program may use at most 64 MiB of HBM per device.

```python
import math
import jax
import jax.numpy as jnp
import numpy as np
from jax import lax

MODEL_WIDTH = 8192
HEAD_WIDTH = 128
KEY_VALUE_HEADS = 4
R = 64
SEGMENT_TOKENS = 128
ADAPTERS = 128
BATCH_TOKENS = 1024
SEGMENT_COUNT = 8


def draw_hidden(key, part):
    key = jax.random.fold_in(key, 17)
    key_base, key_rows, key_cols = jax.random.split(key, 3)
    col_scale = jnp.exp(jax.random.uniform(key_cols, (1, MODEL_WIDTH), jnp.float32) * math.log(10.0))
    row_scale = jnp.exp(jax.random.uniform(key_rows, (BATCH_TOKENS, 1), jnp.float32) * math.log(10.0))
    core_part = jnp.clip(jax.random.normal(key_base, (BATCH_TOKENS, MODEL_WIDTH), jnp.float32), -6.0, 6.0)
    return (core_part * row_scale * col_scale).astype(jnp.bfloat16)


def place_ends(values, key, low, largest):
    longest = values.shape.index(max(values.shape))
    spots = []
    for shift in (0, 1):
        where = [jax.random.randint(jax.random.fold_in(key, axis), (), 0, length) for axis, length in enumerate(values.shape)]
        where[longest] = (where[longest] + shift) % values.shape[longest]
        spots.append(tuple(where))
    return values.at[spots[0]].set(low).at[spots[1]].set(largest)


def levels(key, extent, shards, least, largest):
    gain, own = 1.0, jax.random.fold_in(key, 6)
    for position, shards_of in shards:
        heights = jnp.exp(jax.random.uniform(jax.random.fold_in(own, position), (shards_of,), jnp.float32, least / len(shards), largest / len(shards)))
        gain = gain * jnp.repeat(heights, extent[position] // shards_of).reshape([-1 if axis == position else 1 for axis in range(len(extent))])
    return gain


def rank_table(number_of, skew):
    loads = [(1 << 20) // math.isqrt(grade ** skew) + 1 for grade in range(1, number_of + 1)]
    spread = 1 + sum(loads) // (1 << 30)
    return np.cumsum(np.array([max(1, weight // spread) for weight in loads]))


def skewed_ids(own_key, extent, count, slope):
    table = rank_table(count, slope)
    pick = jax.random.randint(jax.random.fold_in(own_key, 1), extent, 0, int(table[count - 1]))
    rank = jnp.searchsorted(jnp.asarray(table, jnp.int32), pick, side="right")
    return jax.random.permutation(jax.random.fold_in(own_key, 2), count)[rank].astype(jnp.int32)


def noise(rng, shape, deviation, most, pieces=(), kind=jnp.bfloat16):
    gain = levels(rng, shape, pieces, -0.22, 0.18) if pieces else 1.0
    result = jax.random.normal(rng, shape, jnp.float32) * deviation * gain
    return jnp.minimum(jnp.maximum(result, -most), most).astype(kind)


def setup_inputs(seed: int = 0, part: int = 0) -> dict:
    arg_keys = jax.random.split(jax.random.key(seed), 8)
    part_splits = jax.random.split(jax.random.fold_in(arg_keys[7], part), 8)
    return {
        "hidden": draw_hidden(jax.random.fold_in(jax.random.fold_in(arg_keys[7], part), 71), part),
        "norm_gain": jnp.clip(1.0 + 0.15 * jax.random.normal(arg_keys[1], (MODEL_WIDTH,), jnp.float32), 0.25, 1.75).astype(jnp.bfloat16),
        "kv_weight": noise(arg_keys[2], (MODEL_WIDTH, 2 * KEY_VALUE_HEADS * HEAD_WIDTH), MODEL_WIDTH ** -0.5, 0.0625, ((0, 8), (1, 2))),
        "down_panels": noise(part_splits[3], (ADAPTERS, 2, MODEL_WIDTH // 2, R), MODEL_WIDTH ** -0.5, 0.0625, ((1, 2), (2, 8))),
        "up_panels": noise(part_splits[4], (ADAPTERS, 2, R * KEY_VALUE_HEADS * HEAD_WIDTH), R ** -0.5, 0.75, ((1, 2), (2, 8))),
        "seg_adapter": place_ends(skewed_ids(part_splits[5], (SEGMENT_COUNT,), ADAPTERS, 2), jax.random.fold_in(part_splits[5], 3), 0, ADAPTERS - 1).astype(jnp.int32),
        "slot_of": jax.random.permutation(part_splits[6], ADAPTERS).astype(jnp.int32),
    }


def reference(hidden, norm_gain, kv_weight, down_panels, up_panels, seg_adapter, slot_of):
    values = hidden.astype(jnp.float32)
    mean_sq = lax.optimization_barrier(jnp.mean(values * values, axis=1, keepdims=True))
    normed_input = (values * lax.rsqrt(mean_sq + 1e-05) * norm_gain.astype(jnp.float32)).astype(jnp.bfloat16)
    base_output = jnp.dot(normed_input, kv_weight, preferred_element_type=jnp.float32)
    slot_indices = slot_of[seg_adapter].astype(jnp.int32)
    down_full = down_panels.reshape(ADAPTERS, MODEL_WIDTH, R)
    up_full = up_panels.reshape(ADAPTERS, 2, R, KEY_VALUE_HEADS * HEAD_WIDTH).transpose(0, 2, 1, 3).reshape(ADAPTERS, R, 2 * KEY_VALUE_HEADS * HEAD_WIDTH)

    def single_segment(segment_item):
        segment_x, slot_id = segment_item
        low_rank = jnp.dot(segment_x, down_full[slot_id], preferred_element_type=jnp.float32).astype(jnp.bfloat16)
        return jnp.dot(low_rank, up_full[slot_id], preferred_element_type=jnp.float32)
    adapter_update = lax.map(single_segment, (normed_input.reshape(SEGMENT_COUNT, SEGMENT_TOKENS, MODEL_WIDTH), slot_indices))
    return (base_output + adapter_update.reshape(BATCH_TOKENS, 2 * KEY_VALUE_HEADS * HEAD_WIDTH)).astype(jnp.bfloat16)
```

```python
import functools

import jax
import jax.numpy as jnp
from jax import lax
from jax.experimental import pallas as pl
from jax.experimental.pallas import tpu as pltpu
from jax.sharding import PartitionSpec as P

SEGMENT_TOKENS = 128
EPS = 1e-05
VMEM_LIMIT = 48 * 1024 * 1024
PAD_ROWS = 16


def params():
    return pltpu.CompilerParams(vmem_limit_bytes=VMEM_LIMIT)


def gather_kernel(peers, place, seg, slot_of, down, up, *rest):
    outs, sem = rest[:peers], rest[peers]
    me = place[0]
    rank, feats = down.shape[1:]
    up_rows = up.shape[1] // feats
    copies = []
    row = lax.broadcasted_iota(jnp.int32, (PAD_ROWS, up.shape[0]), 0)
    col = lax.broadcasted_iota(jnp.int32, (PAD_ROWS, up.shape[0]), 1)
    hot = jnp.zeros((PAD_ROWS, up.shape[0]), jnp.float32)
    for k in range(peers):
        slot = slot_of[seg[me ^ k]]
        copy = pltpu.make_async_copy(down.at[slot], outs[k].at[pl.ds(0, rank)], sem.at[k])
        copy.start()
        copies.append(copy)
        hot = jnp.where((row == k) & (col == slot), 1.0, hot)
    picked = jnp.dot(hot.astype(jnp.bfloat16), up[...], preferred_element_type=jnp.float32)
    for k in range(peers):
        rows = [picked[k : k + 1, r * feats : (r + 1) * feats] for r in range(up_rows)]
        rows.append(jnp.zeros((PAD_ROWS - up_rows, feats), jnp.float32))
        outs[k][pl.ds(rank, PAD_ROWS), :] = jnp.concatenate(rows, axis=0).astype(jnp.bfloat16)
    for copy in copies:
        copy.wait()


def norm_send_kernel(chunks, place, hidden, gain, out):
    side = place[1]
    values = hidden[...].astype(jnp.float32)
    inv = lax.rsqrt(jnp.mean(values * values, axis=1, keepdims=True) + EPS)
    half = hidden.shape[1] // 2
    chunk = half // chunks
    for part in range(2):
        first = (side if part == 0 else 1 - side) * half
        for q in range(chunks):
            at = pl.ds(pl.multiple_of(first + q * chunk, chunk), chunk)
            piece = hidden[:, at].astype(jnp.float32) * inv * gain[:, at].astype(jnp.float32)
            out[q, :, part * chunk : (part + 1) * chunk] = piece.astype(jnp.bfloat16)


def norm_half_kernel(place, hidden, gain, out):
    values = hidden[...].astype(jnp.float32)
    inv = lax.rsqrt(jnp.mean(values * values, axis=1, keepdims=True) + EPS)
    half = hidden.shape[1] // 2
    at = pl.ds(pl.multiple_of(place[2] * half, half), half)
    out[...] = (hidden[:, at].astype(jnp.float32) * inv * gain[:, at].astype(jnp.float32)).astype(jnp.bfloat16)


def partial_kernel(place, mine, other, own_w, far_w, out):
    half = place[2]
    rows = mine.shape[1]
    chunk = own_w.shape[0]
    for part, acts in ((0, mine), (1, other)):
        x = acts[0]
        total = jnp.dot(x[:, :chunk], own_w[...], preferred_element_type=jnp.float32)
        total += jnp.dot(x[:, chunk:], far_w[...], preferred_element_type=jnp.float32)
        at = (half if part == 0 else 1 - half) * rows
        out[0, pl.ds(pl.multiple_of(at, rows), rows), :] = total.astype(jnp.bfloat16)


def rank_kernel(peers, place, acts, *rest):
    pieces, out = rest[:peers], rest[peers]
    me = place[0]
    rank = out.shape[1]
    feats = pieces[0].shape[1]
    total = jnp.zeros(out.shape, jnp.float32)
    for k in range(peers):
        x = acts[:, pl.ds(pl.multiple_of((me ^ k) * feats, feats), feats)]
        total += lax.dot_general(x, pieces[k][:rank, :], (((1,), (1,)), ((), ())), preferred_element_type=jnp.float32)
    out[...] = total


def final_kernel(peers, up_rows, place, parts, low_mine, low_other, *rest):
    pieces, out, up_full = rest[:peers], rest[peers], rest[peers + 1]
    me = place[0]
    rank = low_mine.shape[1]
    for k in range(peers):
        at = pl.ds(pl.multiple_of((me ^ k) * up_rows, up_rows), up_rows)
        up_full[at, :] = pieces[k][rank : rank + PAD_ROWS, :].astype(jnp.float32)[:up_rows]
    low = (low_mine[...] + low_other[...]).astype(jnp.bfloat16)
    total = jnp.dot(low, up_full[...].astype(jnp.bfloat16), preferred_element_type=jnp.float32)
    for q in range(parts.shape[0]):
        total += parts[q].astype(jnp.float32)
    out[...] = total.astype(jnp.bfloat16)


def whole(shape):
    return pl.BlockSpec(shape, lambda *_: (0,) * len(shape))


def call(kernel, prefetch, args, in_specs, outs, out_specs, grid=(1,), scratch=(), name=None, flops=0, nbytes=0):
    return pl.pallas_call(
        kernel,
        grid_spec=pltpu.PrefetchScalarGridSpec(
            num_scalar_prefetch=len(prefetch),
            grid=grid,
            in_specs=in_specs,
            out_specs=out_specs,
            scratch_shapes=scratch,
        ),
        out_shape=outs,
        compiler_params=params(),
        cost_estimate=pl.CostEstimate(flops=flops, bytes_accessed=nbytes, transcendentals=0),
        name=name,
    )(*prefetch, *args)


def cube_device(hidden, norm_gain, kv_weight, down_panels, up_panels, seg_adapter, slot_of):
    tokens, features = hidden.shape
    groups, peers = lax.axis_size("groups"), lax.axis_size("tensor")
    g, t, h = (lax.axis_index(axis) for axis in ("groups", "tensor", "pool"))
    lows = peers // 2
    cube = groups * lows
    chunk = kv_weight.shape[0] // groups
    cols = kv_weight.shape[1]
    rows = tokens // 2
    feats, rank = down_panels.shape[2:]
    bf16, f32 = jnp.bfloat16, jnp.float32
    place = jnp.stack([t, t // lows, h]).astype(jnp.int32)
    swap = [(i, i ^ lows) for i in range(peers)]
    cubes = [[a * peers + s * lows + l for l in range(lows) for a in range(groups)] for s in range(2)]
    gain = norm_gain.reshape(1, features)
    up_rows = up_panels.shape[2] // feats

    own_w = lax.dynamic_slice_in_dim(kv_weight, g * chunk, chunk, 0)
    far_w = lax.ppermute(own_w, "tensor", swap)

    send = call(
        functools.partial(norm_send_kernel, cube), [place], [hidden, gain],
        [pl.BlockSpec((rows, features), lambda i, p: (p[2], 0)), whole((1, features))],
        jax.ShapeDtypeStruct((cube, rows, 2 * chunk), bf16), whole((cube, rows, 2 * chunk)),
        name="norm_send", flops=6 * rows * features, nbytes=4 * rows * features,
    )
    mine = lax.all_to_all(
        send, ("groups", "tensor"), split_axis=0, concat_axis=0, tiled=True, axis_index_groups=cubes
    )

    piece_shape = (rank + PAD_ROWS, feats)
    pieces = call(
        functools.partial(gather_kernel, peers), [place, seg_adapter, slot_of],
        [down_panels[:, 0].transpose(0, 2, 1), up_panels[:, 0]],
        [pl.BlockSpec(memory_space=pl.ANY), whole((up_panels.shape[0], up_panels.shape[2]))],
        [jax.ShapeDtypeStruct(piece_shape, bf16)] * peers, [whole(piece_shape)] * peers,
        scratch=[pltpu.SemaphoreType.DMA((peers,))], name="pick_panels", nbytes=3 << 20,
    )
    pieces = [pieces[0]] + [
        lax.ppermute(pieces[k], "tensor", [(i, i ^ k) for i in range(peers)]) for k in range(1, peers)
    ]
    acts = call(
        norm_half_kernel, [place], [hidden, gain], [whole((tokens, features)), whole((1, features))],
        jax.ShapeDtypeStruct((tokens, features // 2), bf16), whole((tokens, features // 2)),
        name="norm_half", flops=6 * tokens * features, nbytes=4 * tokens * features,
    )

    other = lax.ppermute(mine, "pool", [(0, 1), (1, 0)])
    block = pl.BlockSpec((1, rows, 2 * chunk), lambda i, p: (i, 0, 0))
    partial = call(
        partial_kernel, [place], [mine, other, own_w, far_w],
        [block, block, whole((chunk, cols)), whole((chunk, cols))],
        jax.ShapeDtypeStruct((cube, tokens, cols), bf16),
        pl.BlockSpec((1, tokens, cols), lambda i, p: (i, 0, 0)), grid=(cube,),
        name="partial", flops=4 * cube * tokens * chunk * cols, nbytes=4 << 20,
    )
    parts = lax.all_to_all(
        partial, ("groups", "tensor"), split_axis=0, concat_axis=0, tiled=True, axis_index_groups=cubes
    )

    low_mine = call(
        functools.partial(rank_kernel, peers), [place], [acts, *pieces],
        [whole(acts.shape)] + [whole(piece_shape)] * peers,
        jax.ShapeDtypeStruct((tokens, rank), f32), whole((tokens, rank)),
        name="low_rank", flops=2 * tokens * rank * features // 2, nbytes=2 << 20,
    )
    low_other = lax.ppermute(low_mine, "pool", [(0, 1), (1, 0)])
    return call(
        functools.partial(final_kernel, peers, up_rows), [place], [parts, low_mine, low_other, *pieces],
        [whole(parts.shape), whole((tokens, rank)), whole((tokens, rank))] + [whole(piece_shape)] * peers,
        jax.ShapeDtypeStruct((tokens, cols), bf16), whole((tokens, cols)),
        scratch=[pltpu.VMEM((rank, cols), f32)], name="final", flops=4 * tokens * rank * cols, nbytes=3 << 20,
    )


def gathered_device(hidden, norm_gain, kv_weight, down_panels, up_panels, seg_adapter, slot_of):
    tok_rows = hidden.shape[0]
    half_width = hidden.shape[1] // 2
    peer_count = lax.axis_size("tensor")
    my_half = lax.axis_index("pool")
    seg_local = tok_rows // SEGMENT_TOKENS
    values = hidden.astype(jnp.float32)
    inv_rms = lax.rsqrt(jnp.mean(values * values, axis=1, keepdims=True) + EPS)
    normed = (values * inv_rms * norm_gain.astype(jnp.float32)).astype(jnp.bfloat16)
    weight = lax.all_gather(kv_weight, "tensor", axis=0, tiled=True)
    base = jnp.dot(normed, weight, preferred_element_type=jnp.float32)
    wanted = slot_of[seg_adapter].reshape(peer_count, seg_local).T
    down_store, up_store = down_panels[:, 0], up_panels[:, 0]
    rank_width = down_store.shape[2]
    normed_half = lax.dynamic_slice_in_dim(normed, my_half * half_width, half_width, 1)
    got_down = lax.all_to_all(down_store[wanted], "tensor", split_axis=1, concat_axis=1, tiled=True)
    up_mats = lax.all_to_all(up_store[wanted], "tensor", split_axis=1, concat_axis=1, tiled=True)
    low_rank = jnp.einsum(
        "sti,sir->str",
        normed_half.reshape(seg_local, SEGMENT_TOKENS, half_width),
        got_down.reshape(seg_local, half_width, rank_width),
        preferred_element_type=jnp.float32,
    )
    low_rank = lax.psum(low_rank, "pool").astype(jnp.bfloat16)
    update = jnp.einsum(
        "str,srh->sth",
        low_rank,
        up_mats.reshape(seg_local, rank_width, -1),
        preferred_element_type=jnp.float32,
    )
    return (base + update.reshape(tok_rows, -1)).astype(jnp.bfloat16)


def per_device(hidden, norm_gain, kv_weight, down_panels, up_panels, seg_adapter, slot_of):
    peers, groups = lax.axis_size("tensor"), lax.axis_size("groups")
    feats = down_panels.shape[2]
    fits = (
        hidden.shape[0] == SEGMENT_TOKENS
        and lax.axis_size("pool") == 2
        and peers in (2, 4, 8)
        and kv_weight.shape[0] % (128 * groups) == 0
        and feats == kv_weight.shape[1]
        and up_panels.shape[2] % (8 * feats) == 0
        and up_panels.shape[2] // feats <= PAD_ROWS
    )
    body = cube_device if fits else gathered_device
    return body(hidden, norm_gain, kv_weight, down_panels, up_panels, seg_adapter, slot_of)


def solution(mesh):
    placed = (
        P(("groups", "tensor"), None),
        P(),
        P("tensor", "pool"),
        P("groups", "pool", "tensor", None),
        P("groups", "pool", "tensor"),
        P("groups"),
        P("groups"),
    )
    return jax.shard_map(
        per_device,
        mesh=mesh,
        in_specs=placed,
        out_specs=P(("groups", "tensor"), "pool"),
        check_vma=False,
    )
```

```python
import functools

import jax
import jax.numpy as jnp
from jax import lax
from jax.experimental import pallas as pl
from jax.experimental.pallas import tpu as pltpu
from jax.sharding import PartitionSpec as P

SEGMENT_TOKENS = 128
EPS = 1e-05
VMEM_LIMIT = 16 * 1024 * 1024
PAD_ROWS = 16
LONG = 1 << 36


def params():
    return pltpu.CompilerParams(vmem_limit_bytes=VMEM_LIMIT)


def gather_kernel(peers, place, seg, slot_of, down, up, *rest):
    outs, sem = rest[:peers], rest[peers]
    me = place[0]
    rank, feats = down.shape[1:]
    up_rows = up.shape[1] // feats
    copies = []
    row = lax.broadcasted_iota(jnp.int32, (PAD_ROWS, up.shape[0]), 0)
    col = lax.broadcasted_iota(jnp.int32, (PAD_ROWS, up.shape[0]), 1)
    hot = jnp.zeros((PAD_ROWS, up.shape[0]), jnp.float32)
    for k in range(peers):
        slot = slot_of[seg[me ^ k]]
        copy = pltpu.make_async_copy(down.at[slot], outs[k].at[pl.ds(0, rank)], sem.at[k])
        copy.start()
        copies.append(copy)
        hot = jnp.where((row == k) & (col == slot), 1.0, hot)
    picked = jnp.dot(hot.astype(jnp.bfloat16), up[...], preferred_element_type=jnp.float32)
    for k in range(peers):
        rows = [picked[k : k + 1, r * feats : (r + 1) * feats] for r in range(up_rows)]
        rows.append(jnp.zeros((PAD_ROWS - up_rows, feats), jnp.float32))
        outs[k][pl.ds(rank, PAD_ROWS), :] = jnp.concatenate(rows, axis=0).astype(jnp.bfloat16)
    for copy in copies:
        copy.wait()


def norm_send_kernel(chunks, place, hidden, gain, out):
    side = place[1]
    values = hidden[...].astype(jnp.float32)
    inv = lax.rsqrt(jnp.mean(values * values, axis=1, keepdims=True) + EPS)
    half = hidden.shape[1] // 2
    chunk = half // chunks
    for part in range(2):
        first = (side if part == 0 else 1 - side) * half
        for q in range(chunks):
            at = pl.ds(pl.multiple_of(first + q * chunk, chunk), chunk)
            piece = hidden[:, at].astype(jnp.float32) * inv * gain[at].astype(jnp.float32)[None, :]
            out[q, :, part * chunk : (part + 1) * chunk] = piece.astype(jnp.bfloat16)


def norm_half_kernel(place, hidden, gain, out):
    values = hidden[...].astype(jnp.float32)
    inv = lax.rsqrt(jnp.mean(values * values, axis=1, keepdims=True) + EPS)
    half = hidden.shape[1] // 2
    at = pl.ds(pl.multiple_of(place[2] * half, half), half)
    out[...] = (hidden[:, at].astype(jnp.float32) * inv * gain[at].astype(jnp.float32)[None, :]).astype(jnp.bfloat16)


def partial_kernel(place, acts, own_w, far_w, *rest):
    out = rest[-1]
    x = acts[0]
    chunk = own_w.shape[0]
    total = jnp.dot(x[:, :chunk], own_w[...], preferred_element_type=jnp.float32)
    total += jnp.dot(x[:, chunk:], far_w[...], preferred_element_type=jnp.float32)
    out[0] = total.astype(jnp.bfloat16)


def rank_kernel(peers, place, acts, *rest):
    pieces, out = rest[:peers], rest[peers]
    me = place[0]
    rank = out.shape[1]
    feats = pieces[0].shape[1]
    total = jnp.zeros(out.shape, jnp.float32)
    for k in range(peers):
        x = acts[:, pl.ds(pl.multiple_of((me ^ k) * feats, feats), feats)]
        total += lax.dot_general(x, pieces[k][:rank, :], (((1,), (1,)), ((), ())), preferred_element_type=jnp.float32)
    out[...] = total


def final_kernel(peers, up_rows, place, parts, low_mine, low_other, *rest):
    pieces, out, up_full = rest[:peers], rest[peers], rest[peers + 1]
    me = place[0]
    rank = low_mine.shape[1]
    for k in range(peers):
        at = pl.ds(pl.multiple_of((me ^ k) * up_rows, up_rows), up_rows)
        up_full[at, :] = pieces[k][rank : rank + PAD_ROWS, :].astype(jnp.float32)[:up_rows]
    low = (low_mine[...] + low_other[...]).astype(jnp.bfloat16)
    total = jnp.dot(low, up_full[...].astype(jnp.bfloat16), preferred_element_type=jnp.float32)
    for q in range(parts.shape[0]):
        total += parts[q].astype(jnp.float32)
    out[...] = total.astype(jnp.bfloat16)


def whole(shape):
    return pl.BlockSpec(shape, lambda *_: (0,) * len(shape))


def call(kernel, prefetch, args, in_specs, outs, out_specs, grid=(1,), scratch=(), alias=None, name=None, flops=0, nbytes=0):
    return pl.pallas_call(
        kernel,
        grid_spec=pltpu.PrefetchScalarGridSpec(
            num_scalar_prefetch=len(prefetch),
            grid=grid,
            in_specs=in_specs,
            out_specs=out_specs,
            scratch_shapes=scratch,
        ),
        out_shape=outs,
        compiler_params=params(),
        input_output_aliases=alias or {},
        cost_estimate=pl.CostEstimate(flops=flops, bytes_accessed=nbytes, transcendentals=0),
        name=name,
    )(*prefetch, *args)


def cube_device(hidden, norm_gain, kv_weight, down_panels, up_panels, seg_adapter, slot_of):
    tokens, features = hidden.shape
    groups, peers = lax.axis_size("groups"), lax.axis_size("tensor")
    g, t, h = (lax.axis_index(axis) for axis in ("groups", "tensor", "pool"))
    lows = peers // 2
    cube = groups * lows
    chunk = kv_weight.shape[0] // groups
    cols = kv_weight.shape[1]
    rows = tokens // 2
    feats, rank = down_panels.shape[2:]
    bf16, f32 = jnp.bfloat16, jnp.float32
    place = jnp.stack([t, t // lows, h]).astype(jnp.int32)
    swap = [(i, i ^ lows) for i in range(peers)]
    cubes = [[a * peers + s * lows + l for l in range(lows) for a in range(groups)] for s in range(2)]
    gain = norm_gain
    up_rows = up_panels.shape[2] // feats

    own_w = lax.dynamic_slice_in_dim(kv_weight, g * chunk, chunk, 0)
    far_w = lax.ppermute(own_w, "tensor", swap)

    send = call(
        functools.partial(norm_send_kernel, cube), [place], [hidden, gain],
        [pl.BlockSpec((rows, features), lambda i, p: (p[2], 0)), whole((features,))],
        jax.ShapeDtypeStruct((cube, rows, 2 * chunk), bf16), whole((cube, rows, 2 * chunk)),
        name="norm_send", flops=6 * rows * features, nbytes=4 * rows * features,
    )
    send, later = lax.optimization_barrier((send, place))
    mine = lax.all_to_all(
        send, ("groups", "tensor"), split_axis=0, concat_axis=0, tiled=True, axis_index_groups=cubes
    )

    piece_shape = (rank + PAD_ROWS, feats)
    pieces = call(
        functools.partial(gather_kernel, peers), [later, seg_adapter, slot_of],
        [down_panels[:, 0].transpose(0, 2, 1), up_panels[:, 0]],
        [pl.BlockSpec(memory_space=pltpu.HBM), whole((up_panels.shape[0], up_panels.shape[2]))],
        [jax.ShapeDtypeStruct(piece_shape, bf16)] * peers, [whole(piece_shape)] * peers,
        scratch=[pltpu.SemaphoreType.DMA((peers,))], name="pick_panels", flops=LONG, nbytes=3 << 20,
    )
    pieces = [pieces[0]] + [
        lax.ppermute(pieces[k], "tensor", [(i, i ^ k) for i in range(peers)]) for k in range(1, peers)
    ]
    acts = call(
        norm_half_kernel, [later], [hidden, gain], [whole((tokens, features)), whole((features,))],
        jax.ShapeDtypeStruct((tokens, features // 2), bf16), whole((tokens, features // 2)),
        name="norm_half", flops=6 * tokens * features, nbytes=4 * tokens * features,
    )

    near = peers // 2
    held = lax.optimization_barrier((mine, far_w, acts, *pieces[:near]))
    mine, far_w, acts = held[:3]
    pieces[:near] = held[3:]
    other = lax.ppermute(mine, "pool", [(0, 1), (1, 0)])
    block = pl.BlockSpec((1, rows, 2 * chunk), lambda i, p: (i, 0, 0))
    weights = [whole((chunk, cols))] * 2
    shape = jax.ShapeDtypeStruct((cube, tokens, cols), bf16)
    work = dict(grid=(cube,), flops=2 * cube * tokens * chunk * cols, nbytes=3 << 20)
    partial = call(
        partial_kernel, [place], [mine, own_w, far_w], [block, *weights], shape,
        pl.BlockSpec((1, rows, cols), lambda i, p: (i, p[2], 0)), name="partial_mine", **work,
    )
    partial = call(
        partial_kernel, [place], [other, own_w, far_w, partial],
        [block, *weights, pl.BlockSpec(memory_space=pl.ANY)], shape,
        pl.BlockSpec((1, rows, cols), lambda i, p: (i, 1 - p[2], 0)), alias={4: 0}, name="partial_other", **work,
    )
    parts = lax.all_to_all(
        partial, ("groups", "tensor"), split_axis=0, concat_axis=0, tiled=True, axis_index_groups=cubes
    )

    low_mine = call(
        functools.partial(rank_kernel, peers), [place], [acts, *pieces],
        [whole(acts.shape)] + [whole(piece_shape)] * peers,
        jax.ShapeDtypeStruct((tokens, rank), f32), whole((tokens, rank)),
        name="low_rank", flops=2 * tokens * rank * features // 2, nbytes=2 << 20,
    )
    low_other = lax.ppermute(low_mine, "pool", [(0, 1), (1, 0)])
    return call(
        functools.partial(final_kernel, peers, up_rows), [place], [parts, low_mine, low_other, *pieces],
        [whole(parts.shape), whole((tokens, rank)), whole((tokens, rank))] + [whole(piece_shape)] * peers,
        jax.ShapeDtypeStruct((tokens, cols), bf16), whole((tokens, cols)),
        scratch=[pltpu.VMEM((rank, cols), f32)], name="final", flops=4 * tokens * rank * cols, nbytes=3 << 20,
    )


def gathered_device(hidden, norm_gain, kv_weight, down_panels, up_panels, seg_adapter, slot_of):
    tok_rows = hidden.shape[0]
    half_width = hidden.shape[1] // 2
    peer_count = lax.axis_size("tensor")
    my_half = lax.axis_index("pool")
    seg_local = tok_rows // SEGMENT_TOKENS
    values = hidden.astype(jnp.float32)
    inv_rms = lax.rsqrt(jnp.mean(values * values, axis=1, keepdims=True) + EPS)
    normed = (values * inv_rms * norm_gain.astype(jnp.float32)).astype(jnp.bfloat16)
    weight = lax.all_gather(kv_weight, "tensor", axis=0, tiled=True)
    base = jnp.dot(normed, weight, preferred_element_type=jnp.float32)
    wanted = slot_of[seg_adapter].reshape(peer_count, seg_local).T
    down_store, up_store = down_panels[:, 0], up_panels[:, 0]
    rank_width = down_store.shape[2]
    normed_half = lax.dynamic_slice_in_dim(normed, my_half * half_width, half_width, 1)
    got_down = lax.all_to_all(down_store[wanted], "tensor", split_axis=1, concat_axis=1, tiled=True)
    up_mats = lax.all_to_all(up_store[wanted], "tensor", split_axis=1, concat_axis=1, tiled=True)
    low_rank = jnp.einsum(
        "sti,sir->str",
        normed_half.reshape(seg_local, SEGMENT_TOKENS, half_width),
        got_down.reshape(seg_local, half_width, rank_width),
        preferred_element_type=jnp.float32,
    )
    low_rank = lax.psum(low_rank, "pool").astype(jnp.bfloat16)
    update = jnp.einsum(
        "str,srh->sth",
        low_rank,
        up_mats.reshape(seg_local, rank_width, -1),
        preferred_element_type=jnp.float32,
    )
    return (base + update.reshape(tok_rows, -1)).astype(jnp.bfloat16)


def per_device(hidden, norm_gain, kv_weight, down_panels, up_panels, seg_adapter, slot_of):
    peers, groups = lax.axis_size("tensor"), lax.axis_size("groups")
    feats = down_panels.shape[2]
    fits = (
        hidden.shape[0] == SEGMENT_TOKENS
        and lax.axis_size("pool") == 2
        and peers in (2, 4, 8)
        and kv_weight.shape[0] % (128 * groups) == 0
        and feats == kv_weight.shape[1]
        and up_panels.shape[2] % (8 * feats) == 0
        and up_panels.shape[2] // feats <= PAD_ROWS
    )
    body = cube_device if fits else gathered_device
    return body(hidden, norm_gain, kv_weight, down_panels, up_panels, seg_adapter, slot_of)


def solution(mesh):
    placed = (
        P(("groups", "tensor"), None),
        P(),
        P("tensor", "pool"),
        P("groups", "pool", "tensor", None),
        P("groups", "pool", "tensor"),
        P("groups"),
        P("groups"),
    )
    return jax.shard_map(
        per_device,
        mesh=mesh,
        in_specs=placed,
        out_specs=P(("groups", "tensor"), "pool"),
        check_vma=False,
    )
```

```python
import functools

import jax
import jax.numpy as jnp
from jax import lax
from jax.experimental import pallas as pl
from jax.experimental.pallas import tpu as pltpu
from jax.sharding import PartitionSpec as P

SEGMENT_TOKENS = 128
EPS = 1e-05
VMEM_LIMIT = 16 * 1024 * 1024
PAD_ROWS = 16
LONG = 1 << 36
PEERS = ((1, 0), (0, 1), (1, 1))


def params():
    return pltpu.CompilerParams(vmem_limit_bytes=VMEM_LIMIT)


def gather_kernel(place, seg, slot_of, down, up, out, sem):
    peers = out.shape[0]
    rank, feats = down.shape[1:]
    up_rows = up.shape[1] // feats
    copies = []
    row = lax.broadcasted_iota(jnp.int32, (PAD_ROWS, up.shape[0]), 0)
    col = lax.broadcasted_iota(jnp.int32, (PAD_ROWS, up.shape[0]), 1)
    hot = jnp.zeros((PAD_ROWS, up.shape[0]), jnp.float32)
    for k in range(peers):
        slot = slot_of[seg[k]]
        copy = pltpu.make_async_copy(down.at[slot], out.at[k, pl.ds(0, rank)], sem.at[k])
        copy.start()
        copies.append(copy)
        hot = jnp.where((row == k) & (col == slot), 1.0, hot)
    picked = jnp.dot(hot.astype(jnp.bfloat16), up[...], preferred_element_type=jnp.float32)
    for k in range(peers):
        rows = [picked[k : k + 1, r * feats : (r + 1) * feats] for r in range(up_rows)]
        rows.append(jnp.zeros((PAD_ROWS - up_rows, feats), jnp.float32))
        out[k, pl.ds(rank, PAD_ROWS), :] = jnp.concatenate(rows, axis=0).astype(jnp.bfloat16)
    for copy in copies:
        copy.wait()


def wanted(place, peer, step, row_count, chunk):
    shard = (place[1] * 2 + peer % 2) ^ (2 * step)
    return pl.multiple_of(shard * row_count + (peer // 2) * chunk, chunk)


def normed_piece(rows, gain, inv, at):
    return (rows[:, at].astype(jnp.float32) * inv * gain[at].astype(jnp.float32)[None, :]).astype(jnp.bfloat16)


def inv_rms(rows):
    values = rows[...].astype(jnp.float32)
    return lax.rsqrt(jnp.mean(values * values, axis=1, keepdims=True) + EPS)


def norm_send_kernel(steps, row_count, chunk, place, hidden, gain_hbm, out, held, gain, sem):
    rows = held.shape[0]
    cut = rows // 4
    first = place[2] * rows
    copies = [pltpu.make_async_copy(gain_hbm, gain, sem.at[4])]
    for i in range(4):
        at = pl.ds(pl.multiple_of(first + i * cut, cut), cut)
        copies.append(pltpu.make_async_copy(hidden.at[at], held.at[pl.ds(i * cut, cut)], sem.at[i]))
    for copy in copies:
        copy.start()
    copies[0].wait()
    for i in range(4):
        copies[1 + i].wait()
        part = held.at[pl.ds(i * cut, cut)]
        inv = inv_rms(part)
        for peer in range(4):
            for step in range(steps):
                at = pl.ds(wanted(place, peer, step, row_count, chunk), chunk)
                out[peer, pl.ds(i * cut, cut), step * chunk : (step + 1) * chunk] = normed_piece(part, gain, inv, at)


def norm_half_kernel(place, hidden, gain, out, held, sem):
    half = hidden.shape[1] // 2
    at = pl.ds(pl.multiple_of(place[2] * half, half), half)
    held[...] = normed_piece(hidden, gain, inv_rms(hidden), at)
    copy = pltpu.make_async_copy(held, out, sem)
    copy.start()
    copy.wait()


def in_order(place, mine, other):
    me = place[3] * 2 + place[0] % 2
    quarters = [me ^ 1, me ^ 2, me ^ 3, me]
    return jnp.concatenate([mine[q] for q in quarters] + [other[q] for q in quarters], axis=0)


def early_kernel(place, mine, other, *rest):
    weights, out = rest[:-1], rest[-1]
    x = in_order(place, mine, other)
    total = jnp.zeros(out.shape, jnp.float32)
    first = 0
    for w in weights:
        total += jnp.dot(x[:, first : first + w.shape[0]], w[...], preferred_element_type=jnp.float32)
        first += w.shape[0]
    out[...] = total


def late_kernel(place, mine, other, weight, early, out0, out1, out2, own):
    rows = mine.shape[1]
    x = in_order(place, mine, other)
    total = early[...] + jnp.dot(x, weight[...], preferred_element_type=jnp.float32)
    half = place[2]
    for part in range(2):
        at = pl.ds(pl.multiple_of((half if part == 0 else 1 - half) * rows, rows), rows)
        for k, out in enumerate((out0, out1, out2, own)):
            first = (4 * part + k) * rows
            out[at, :] = total[first : first + rows].astype(out.dtype)


def rank_kernel(place, acts, pieces, out):
    rank = out.shape[1]
    feats = pieces.shape[2]
    total = jnp.zeros(out.shape, jnp.float32)
    for k in range(pieces.shape[0]):
        x = acts[:, k * feats : (k + 1) * feats]
        total += lax.dot_general(x, pieces[k, :rank, :], (((1,), (1,)), ((), ())), preferred_element_type=jnp.float32)
    out[...] = total


def final_kernel(up_rows, place, own, far0, far1, far2, low_mine, low_other, pieces, out):
    rank = low_mine.shape[1]
    up = [pieces[k, rank : rank + PAD_ROWS, :].astype(jnp.float32)[:up_rows] for k in range(pieces.shape[0])]
    low = (low_mine[...] + low_other[...]).astype(jnp.bfloat16)
    up = jnp.concatenate(up, axis=0).astype(jnp.bfloat16)
    total = jnp.dot(low, up, preferred_element_type=jnp.float32) + own[...]
    for part in (far0, far1, far2):
        total += part[...].astype(jnp.float32)
    out[...] = total.astype(jnp.bfloat16)


def whole(shape):
    return pl.BlockSpec(shape, lambda *_: (0,) * len(shape))


def call(kernel, prefetch, args, in_specs, outs, out_specs, grid=(1,), scratch=(), alias=None, name=None, flops=0, nbytes=0):
    return pl.pallas_call(
        kernel,
        grid_spec=pltpu.PrefetchScalarGridSpec(
            num_scalar_prefetch=len(prefetch),
            grid=grid,
            in_specs=in_specs,
            out_specs=out_specs,
            scratch_shapes=scratch,
        ),
        out_shape=outs,
        compiler_params=params(),
        input_output_aliases=alias or {},
        cost_estimate=pl.CostEstimate(flops=flops, bytes_accessed=nbytes, transcendentals=0),
        name=name,
    )(*prefetch, *args)


def square_device(hidden, norm_gain, kv_weight, down_panels, up_panels, seg_adapter, slot_of):
    tokens, features = hidden.shape
    groups, peers = lax.axis_size("groups"), lax.axis_size("tensor")
    g, t, h = (lax.axis_index(axis) for axis in ("groups", "tensor", "pool"))
    steps = peers // 2
    row_count, cols = kv_weight.shape
    chunk = row_count // groups
    rows = tokens // 2
    span = steps * chunk
    feats, rank = down_panels.shape[2:]
    bf16, f32 = jnp.bfloat16, jnp.float32
    place = jnp.stack([t, t // 2, h, g]).astype(jnp.int32)
    up_rows = up_panels.shape[2] // feats
    hbm = pl.BlockSpec(memory_space=pltpu.HBM)
    cores = [(0, 1), (1, 0)]

    def to_peer(x, flip_x, flip_g):
        pairs = [(i, i ^ flip_x ^ (flip_g * peers)) for i in range(groups * peers)]
        return lax.ppermute(x, ("groups", "tensor"), pairs)

    own_w = lax.dynamic_slice_in_dim(kv_weight, g * chunk, chunk, 0)


    def along_z(x, step):
        return lax.ppermute(x, "tensor", [(i, i ^ (2 * step)) for i in range(peers)])

    second = along_z(own_w, 2)
    first = along_z(own_w, 1)
    squares = [[a * peers + z * 2 + x for a in range(groups) for x in range(2)] for z in range(steps)]
    send = call(
        functools.partial(norm_send_kernel, steps, row_count, chunk), [place], [hidden, norm_gain], [hbm, hbm],
        jax.ShapeDtypeStruct((4, rows, span), bf16), whole((4, rows, span)),
        scratch=[pltpu.VMEM((rows, features), bf16), pltpu.VMEM((features,), bf16), pltpu.SemaphoreType.DMA((5,))],
        name="norm_send", flops=6 * rows * features, nbytes=4 * rows * features,
    )
    send, later = lax.optimization_barrier((send, place))
    mine = lax.all_to_all(
        send, ("groups", "tensor"), split_axis=0, concat_axis=0, tiled=True, axis_index_groups=squares
    )

    piece_shape = (peers, rank + PAD_ROWS, feats)
    pieces = call(
        gather_kernel, [later, seg_adapter, slot_of],
        [down_panels[:, 0].transpose(0, 2, 1), up_panels[:, 0]],
        [hbm, whole((up_panels.shape[0], up_panels.shape[2]))],
        jax.ShapeDtypeStruct(piece_shape, bf16), whole(piece_shape),
        scratch=[pltpu.SemaphoreType.DMA((peers,))], name="pick_panels", flops=LONG, nbytes=3 << 20,
    )
    mine, pieces, later, second = lax.optimization_barrier((mine, pieces, later, second))
    third = along_z(second, 1)
    acts = call(
        norm_half_kernel, [later], [hidden, norm_gain], [whole((tokens, features)), whole((features,))],
        jax.ShapeDtypeStruct((tokens, features // 2), bf16), hbm,
        scratch=[pltpu.VMEM((tokens, features // 2), bf16), pltpu.SemaphoreType.DMA], name="norm_half", flops=LONG, nbytes=4 * tokens * features,
    )
    others = [lax.ppermute(mine, "pool", cores)]
    weight = whole((chunk, cols))
    early = call(
        early_kernel, [place], [mine, *others, own_w, first, second],
        [pl.BlockSpec((4, rows, span - chunk), lambda i, p: (0, 0, 0))] * 2 + [weight] * 3,
        jax.ShapeDtypeStruct((4 * tokens, cols), f32), whole((4 * tokens, cols)),
        name="early_rows", flops=24 * tokens * chunk * cols, nbytes=4 << 20,
    )
    acts, early, third = lax.optimization_barrier((acts, early, third))
    late = call(
        late_kernel, [place], [mine, *others, third, early],
        [pl.BlockSpec((4, rows, chunk), lambda i, p: (0, 0, steps - 1))] * 2 + [weight, whole(early.shape)],
        [jax.ShapeDtypeStruct((tokens, cols), bf16)] * 3 + [jax.ShapeDtypeStruct((tokens, cols), f32)],
        [whole((tokens, cols))] * 4,
        name="late_rows", flops=8 * tokens * chunk * cols, nbytes=4 << 20,
    )
    parts = [to_peer(x, *peer) for x, peer in zip(late[:3], PEERS)]

    pieces = lax.all_to_all(pieces, "tensor", split_axis=0, concat_axis=0, tiled=True)
    low_mine = call(
        rank_kernel, [place], [acts, pieces], [whole(acts.shape), whole(piece_shape)],
        jax.ShapeDtypeStruct((tokens, rank), f32), whole((tokens, rank)),
        name="low_rank", flops=2 * tokens * rank * features // 2, nbytes=2 << 20,
    )
    low_other = lax.ppermute(low_mine, "pool", cores)
    return call(
        functools.partial(final_kernel, up_rows), [place],
        [late[3], *parts, low_mine, low_other, pieces],
        [whole((tokens, cols))] * 4 + [whole((tokens, rank))] * 2 + [whole(piece_shape)],
        jax.ShapeDtypeStruct((tokens, cols), bf16), whole((tokens, cols)),
        name="final", flops=4 * tokens * rank * cols, nbytes=3 << 20,
    )


def gathered_device(hidden, norm_gain, kv_weight, down_panels, up_panels, seg_adapter, slot_of):
    tok_rows = hidden.shape[0]
    half_width = hidden.shape[1] // 2
    peer_count = lax.axis_size("tensor")
    my_half = lax.axis_index("pool")
    seg_local = tok_rows // SEGMENT_TOKENS
    values = hidden.astype(jnp.float32)
    inv_rms = lax.rsqrt(jnp.mean(values * values, axis=1, keepdims=True) + EPS)
    normed = (values * inv_rms * norm_gain.astype(jnp.float32)).astype(jnp.bfloat16)
    weight = lax.all_gather(kv_weight, "tensor", axis=0, tiled=True)
    base = jnp.dot(normed, weight, preferred_element_type=jnp.float32)
    wanted = slot_of[seg_adapter].reshape(peer_count, seg_local).T
    down_store, up_store = down_panels[:, 0], up_panels[:, 0]
    rank_width = down_store.shape[2]
    normed_half = lax.dynamic_slice_in_dim(normed, my_half * half_width, half_width, 1)
    got_down = lax.all_to_all(down_store[wanted], "tensor", split_axis=1, concat_axis=1, tiled=True)
    up_mats = lax.all_to_all(up_store[wanted], "tensor", split_axis=1, concat_axis=1, tiled=True)
    low_rank = jnp.einsum(
        "sti,sir->str",
        normed_half.reshape(seg_local, SEGMENT_TOKENS, half_width),
        got_down.reshape(seg_local, half_width, rank_width),
        preferred_element_type=jnp.float32,
    )
    low_rank = lax.psum(low_rank, "pool").astype(jnp.bfloat16)
    update = jnp.einsum(
        "str,srh->sth",
        low_rank,
        up_mats.reshape(seg_local, rank_width, -1),
        preferred_element_type=jnp.float32,
    )
    return (base + update.reshape(tok_rows, -1)).astype(jnp.bfloat16)


def per_device(hidden, norm_gain, kv_weight, down_panels, up_panels, seg_adapter, slot_of):
    peers, groups = lax.axis_size("tensor"), lax.axis_size("groups")
    feats = down_panels.shape[2]
    fits = (
        hidden.shape[0] == SEGMENT_TOKENS
        and lax.axis_size("pool") == 2
        and peers == 8
        and groups == 2
        and kv_weight.shape[0] % (128 * groups) == 0
        and feats == kv_weight.shape[1]
        and up_panels.shape[2] % (8 * feats) == 0
        and up_panels.shape[2] // feats <= PAD_ROWS
    )
    body = square_device if fits else gathered_device
    return body(hidden, norm_gain, kv_weight, down_panels, up_panels, seg_adapter, slot_of)


def solution(mesh):
    placed = (
        P(("groups", "tensor"), None),
        P(),
        P("tensor", "pool"),
        P("groups", "pool", "tensor", None),
        P("groups", "pool", "tensor"),
        P("groups"),
        P("groups"),
    )
    return jax.shard_map(
        per_device,
        mesh=mesh,
        in_specs=placed,
        out_specs=P(("groups", "tensor"), "pool"),
        check_vma=False,
    )
```

```python
import functools

import jax
import jax.numpy as jnp
from jax import lax
from jax.experimental import pallas as pl
from jax.experimental.pallas import tpu as pltpu
from jax.sharding import PartitionSpec as P

SEGMENT_TOKENS = 128
EPS = 1e-05
VMEM_LIMIT = 16 * 1024 * 1024
PAD_ROWS = 8
LONG = 1 << 36
PEERS = ((1, 1), (1, 0), (0, 1))


def params():
    return pltpu.CompilerParams(vmem_limit_bytes=VMEM_LIMIT)


def gather_kernel(seg, slot_of, down, up, out, sem):
    peers = out.shape[0]
    rank, feats = down.shape[1:]
    up_rows = up.shape[1] // feats
    copies = []
    row = lax.broadcasted_iota(jnp.int32, (2 * PAD_ROWS, up.shape[0]), 0)
    col = lax.broadcasted_iota(jnp.int32, (2 * PAD_ROWS, up.shape[0]), 1)
    hot = jnp.zeros((2 * PAD_ROWS, up.shape[0]), jnp.float32)
    for k in range(peers):
        slot = slot_of[seg[k]]
        copy = pltpu.make_async_copy(down.at[slot], out.at[k, pl.ds(0, rank)], sem.at[k])
        copy.start()
        copies.append(copy)
        hot = jnp.where((row == k) & (col == slot), 1.0, hot)
    picked = jnp.dot(hot.astype(jnp.bfloat16), up[...], preferred_element_type=jnp.float32)
    for k in range(peers):
        rows = [picked[k : k + 1, r * feats : (r + 1) * feats] for r in range(up_rows)]
        out[k, pl.ds(rank, PAD_ROWS), :] = jnp.concatenate(rows, axis=0).astype(jnp.bfloat16)
    for copy in copies:
        copy.wait()


def wanted(peer, step, row_count, chunk):
    shard = (lax.axis_index("tensor") // 2 * 2 + peer % 2) ^ (2 * step)
    return pl.multiple_of(shard * row_count + (peer // 2) * chunk, chunk)


def normed_piece(rows, gain, inv, at):
    return (rows[:, at].astype(jnp.float32) * inv * gain[at].astype(jnp.float32)[None, :]).astype(jnp.bfloat16)


def inv_rms(rows):
    values = rows[...].astype(jnp.float32)
    return lax.rsqrt(jnp.mean(values * values, axis=1, keepdims=True) + EPS)


def norm_send_kernel(steps, row_count, chunk, hidden, gain_hbm, out, held, gain, sem):
    rows = held.shape[0]
    cut = rows // 4
    first = lax.axis_index("pool") * rows
    copies = [pltpu.make_async_copy(gain_hbm, gain, sem.at[4])]
    for i in range(4):
        at = pl.ds(pl.multiple_of(first + i * cut, cut), cut)
        copies.append(pltpu.make_async_copy(hidden.at[at], held.at[pl.ds(i * cut, cut)], sem.at[i]))
    for copy in copies:
        copy.start()
    copies[0].wait()
    for i in range(4):
        copies[1 + i].wait()
        part = held.at[pl.ds(i * cut, cut)]
        inv = inv_rms(part)
        for peer in range(4):
            for step in range(steps):
                at = pl.ds(wanted(peer, step, row_count, chunk), chunk)
                out[peer, pl.ds(i * cut, cut), step * chunk : (step + 1) * chunk] = normed_piece(part, gain, inv, at)


def norm_half_kernel(token, hidden, gain, out):
    half = hidden.shape[1] // 2
    at = pl.ds(pl.multiple_of(lax.axis_index("pool") * half, half), half)
    out[...] = normed_piece(hidden, gain, inv_rms(hidden), at)


def tick_kernel(token, out):
    out[...] = token[...]


def in_order(mine, other, cols):
    me = lax.axis_index("groups") * 2 + lax.axis_index("tensor") % 2
    quarters = [me ^ 3, me ^ 1, me ^ 2, me]
    return jnp.concatenate([half[q, :, cols] for half in (mine, other) for q in quarters], axis=0)


def early_kernel(mine, other, *rest):
    weights, out = rest[:-1], rest[-1]
    total = jnp.zeros(out.shape, jnp.float32)
    first = 0
    for w in weights:
        x = in_order(mine, other, slice(first, first + w.shape[0]))
        total += jnp.dot(x, w[...], preferred_element_type=jnp.float32)
        first += w.shape[0]
    out[...] = total


def late_kernel(mine, other, weight, early, out0, out1, out2, own):
    rows = mine.shape[1]
    x = in_order(mine, other, slice(mine.shape[2] - weight.shape[0], mine.shape[2]))
    total = early[...] + jnp.dot(x, weight[...], preferred_element_type=jnp.float32)
    half = lax.axis_index("pool")
    for part in range(2):
        at = pl.ds(pl.multiple_of((half if part == 0 else 1 - half) * rows, rows), rows)
        for k, out in enumerate((out0, out1, out2, own)):
            first = (4 * part + k) * rows
            out[at, :] = total[first : first + rows].astype(out.dtype)


def rank_kernel(acts, pieces, out):
    rank = out.shape[1]
    feats = pieces.shape[2]
    total = jnp.zeros(out.shape, jnp.float32)
    for k in range(pieces.shape[0]):
        x = acts[:, k * feats : (k + 1) * feats]
        total += lax.dot_general(x, pieces[k, :rank, :], (((1,), (1,)), ((), ())), preferred_element_type=jnp.float32)
    out[...] = total


def final_kernel(up_rows, own, far0, far1, far2, low_mine, low_other, pieces, out):
    rank = low_mine.shape[1]
    up = [pieces[k, rank : rank + PAD_ROWS, :].astype(jnp.float32)[:up_rows] for k in range(pieces.shape[0])]
    low = (low_mine[...] + low_other[...]).astype(jnp.bfloat16)
    up = jnp.concatenate(up, axis=0).astype(jnp.bfloat16)
    total = jnp.dot(low, up, preferred_element_type=jnp.float32) + own[...]
    for part in (far0, far1, far2):
        total += part[...].astype(jnp.float32)
    out[...] = total.astype(jnp.bfloat16)


def whole(shape):
    return pl.BlockSpec(memory_space=pltpu.VMEM)


def call(kernel, prefetch, args, in_specs, outs, out_specs, grid=(), scratch=(), alias=None, name=None, flops=0, nbytes=0):
    return pl.pallas_call(
        kernel,
        grid_spec=pltpu.PrefetchScalarGridSpec(
            num_scalar_prefetch=len(prefetch),
            grid=grid,
            in_specs=in_specs,
            out_specs=out_specs,
            scratch_shapes=scratch,
        ),
        out_shape=outs,
        compiler_params=params(),
        input_output_aliases=alias or {},
        cost_estimate=pl.CostEstimate(flops=flops, bytes_accessed=nbytes, transcendentals=0),
        name=name,
    )(*prefetch, *args)


def square_device(hidden, norm_gain, kv_weight, down_panels, up_panels, seg_adapter, slot_of):
    tokens, features = hidden.shape
    groups, peers = lax.axis_size("groups"), lax.axis_size("tensor")
    g = lax.axis_index("groups")
    steps = peers // 2
    row_count, cols = kv_weight.shape
    chunk = row_count // groups
    rows = tokens // 2
    span = steps * chunk
    feats, rank = down_panels.shape[2:]
    bf16, f32 = jnp.bfloat16, jnp.float32
    up_rows = up_panels.shape[2] // feats
    hbm = pl.BlockSpec(memory_space=pltpu.HBM)
    cores = [(0, 1), (1, 0)]

    def to_peer(x, flip_x, flip_g):
        pairs = [(i, i ^ flip_x ^ (flip_g * peers)) for i in range(groups * peers)]
        return lax.ppermute(x, ("groups", "tensor"), pairs)

    own_w = lax.dynamic_slice_in_dim(kv_weight, g * chunk, chunk, 0)


    def along_z(x, step):
        return lax.ppermute(x, "tensor", [(i, i ^ (2 * step)) for i in range(peers)])

    second, first = along_z(own_w, 2), along_z(own_w, 1)
    squares = [[a * peers + z * 2 + x for a in range(groups) for x in range(2)] for z in range(steps)]
    send = call(
        functools.partial(norm_send_kernel, steps, row_count, chunk), [], [hidden, norm_gain], [hbm, hbm],
        jax.ShapeDtypeStruct((4, rows, span), bf16), whole((4, rows, span)),
        scratch=[pltpu.VMEM((rows, features), bf16), pltpu.VMEM((features,), bf16), pltpu.SemaphoreType.DMA((5,))],
        name="norm_send", flops=6 * rows * features, nbytes=4 * rows * features,
    )
    send, later = lax.optimization_barrier((send, slot_of))
    mine = lax.all_to_all(
        send, ("groups", "tensor"), split_axis=0, concat_axis=0, tiled=True, axis_index_groups=squares
    )

    piece_shape = (peers, rank + PAD_ROWS, feats)
    pieces = call(
        gather_kernel, [seg_adapter, later],
        [down_panels[:, 0].transpose(0, 2, 1), up_panels[:, 0]],
        [hbm, whole((up_panels.shape[0], up_panels.shape[2]))],
        jax.ShapeDtypeStruct(piece_shape, bf16), whole(piece_shape),
        scratch=[pltpu.SemaphoreType.DMA((peers,))], name="pick_panels", flops=LONG, nbytes=3 << 20,
    )
    mine, pieces, later, second, first = lax.optimization_barrier((mine, pieces, later, second, first))
    third = along_z(second, 1)
    tick = call(
        tick_kernel, [], [later], [whole(later.shape)], jax.ShapeDtypeStruct(later.shape, jnp.int32),
        whole(later.shape), name="tick", flops=LONG,
    )
    others = [lax.ppermute(mine, "pool", cores)]
    weight = whole((chunk, cols))
    early = call(
        early_kernel, [], [mine, *others, own_w, first, second],
        [weight] * 5,
        jax.ShapeDtypeStruct((4 * tokens, cols), f32), whole((4 * tokens, cols)),
        name="early_rows", flops=24 * tokens * chunk * cols, nbytes=4 << 20,
    )
    early, pieces = lax.optimization_barrier((early, pieces))
    tick, early, third = lax.optimization_barrier((tick, early, third))
    late = call(
        late_kernel, [], [mine, *others, third, early],
        [weight] * 4,
        [jax.ShapeDtypeStruct((tokens, cols), bf16)] * 3 + [jax.ShapeDtypeStruct((tokens, cols), f32)],
        [whole((tokens, cols))] * 4,
        name="late_rows", flops=8 * tokens * chunk * cols, nbytes=4 << 20,
    )
    *late, last = lax.optimization_barrier((*late, tick))
    acts = call(
        norm_half_kernel, [], [last, hidden, norm_gain],
        [pl.BlockSpec(memory_space=pl.ANY), whole((tokens, features)), whole((features,))],
        jax.ShapeDtypeStruct((tokens, features // 2), bf16), whole((tokens, features // 2)),
        name="norm_half", flops=6 * tokens * features, nbytes=4 * tokens * features,
    )
    parts = [to_peer(x, *peer) for x, peer in zip(late[:3], PEERS)]

    pieces = lax.all_to_all(pieces, "tensor", split_axis=0, concat_axis=0, tiled=True)
    low_mine = call(
        rank_kernel, [], [acts, pieces], [whole(acts.shape), whole(piece_shape)],
        jax.ShapeDtypeStruct((tokens, rank), f32), whole((tokens, rank)),
        name="low_rank", flops=2 * tokens * rank * features // 2, nbytes=2 << 20,
    )
    low_other = lax.ppermute(low_mine, "pool", cores)
    return call(
        functools.partial(final_kernel, up_rows), [],
        [late[3], *parts, low_mine, low_other, pieces],
        [whole((tokens, cols))] * 4 + [whole((tokens, rank))] * 2 + [whole(piece_shape)],
        jax.ShapeDtypeStruct((tokens, cols), bf16), whole((tokens, cols)),
        name="final", flops=4 * tokens * rank * cols, nbytes=3 << 20,
    )


def gathered_device(hidden, norm_gain, kv_weight, down_panels, up_panels, seg_adapter, slot_of):
    tok_rows = hidden.shape[0]
    half_width = hidden.shape[1] // 2
    peer_count = lax.axis_size("tensor")
    my_half = lax.axis_index("pool")
    seg_local = tok_rows // SEGMENT_TOKENS
    values = hidden.astype(jnp.float32)
    inv_rms = lax.rsqrt(jnp.mean(values * values, axis=1, keepdims=True) + EPS)
    normed = (values * inv_rms * norm_gain.astype(jnp.float32)).astype(jnp.bfloat16)
    weight = lax.all_gather(kv_weight, "tensor", axis=0, tiled=True)
    base = jnp.dot(normed, weight, preferred_element_type=jnp.float32)
    wanted = slot_of[seg_adapter].reshape(peer_count, seg_local).T
    down_store, up_store = down_panels[:, 0], up_panels[:, 0]
    rank_width = down_store.shape[2]
    normed_half = lax.dynamic_slice_in_dim(normed, my_half * half_width, half_width, 1)
    got_down = lax.all_to_all(down_store[wanted], "tensor", split_axis=1, concat_axis=1, tiled=True)
    up_mats = lax.all_to_all(up_store[wanted], "tensor", split_axis=1, concat_axis=1, tiled=True)
    low_rank = jnp.einsum(
        "sti,sir->str",
        normed_half.reshape(seg_local, SEGMENT_TOKENS, half_width),
        got_down.reshape(seg_local, half_width, rank_width),
        preferred_element_type=jnp.float32,
    )
    low_rank = lax.psum(low_rank, "pool").astype(jnp.bfloat16)
    update = jnp.einsum(
        "str,srh->sth",
        low_rank,
        up_mats.reshape(seg_local, rank_width, -1),
        preferred_element_type=jnp.float32,
    )
    return (base + update.reshape(tok_rows, -1)).astype(jnp.bfloat16)


def per_device(hidden, norm_gain, kv_weight, down_panels, up_panels, seg_adapter, slot_of):
    peers, groups = lax.axis_size("tensor"), lax.axis_size("groups")
    feats = down_panels.shape[2]
    fits = (
        hidden.shape[0] == SEGMENT_TOKENS
        and lax.axis_size("pool") == 2
        and peers == 8
        and groups == 2
        and kv_weight.shape[0] % (128 * groups) == 0
        and feats == kv_weight.shape[1]
        and up_panels.shape[2] % (8 * feats) == 0
        and up_panels.shape[2] // feats == PAD_ROWS
    )
    body = square_device if fits else gathered_device
    return body(hidden, norm_gain, kv_weight, down_panels, up_panels, seg_adapter, slot_of)


def solution(mesh):
    placed = (
        P(("groups", "tensor"), None),
        P(),
        P("tensor", "pool"),
        P("groups", "pool", "tensor", None),
        P("groups", "pool", "tensor"),
        P("groups"),
        P("groups"),
    )
    return jax.shard_map(
        per_device,
        mesh=mesh,
        in_specs=placed,
        out_specs=P(("groups", "tensor"), "pool"),
        check_vma=False,
    )
```

```python
import functools

import jax
import jax.numpy as jnp
from jax import lax
from jax.experimental import pallas as pl
from jax.experimental.pallas import tpu as pltpu
from jax.sharding import PartitionSpec as P

SEGMENT_TOKENS = 128
EPS = 1e-05
VMEM_LIMIT = 16 * 1024 * 1024
PAD_ROWS = 8
LONG = 1 << 36
PEERS = ((1, 1), (1, 0), (0, 1))


def panel_order(peers):
    planes = peers // 2
    inner = [*range(planes // 2, -1, -1), *range(planes // 2 + 1, planes)]
    return [2 * z + x for z in inner for x in range(2)]


def gather_kernel(seg, slot_of, down, up, out, sem):
    peers = out.shape[0]
    rank, feats = down.shape[1:]
    up_rows = up.shape[1] // feats
    copies = []
    row = lax.broadcasted_iota(jnp.int32, (2 * PAD_ROWS, up.shape[0]), 0)
    col = lax.broadcasted_iota(jnp.int32, (2 * PAD_ROWS, up.shape[0]), 1)
    hot = jnp.zeros((2 * PAD_ROWS, up.shape[0]), jnp.float32)
    for k in range(peers):
        slot = slot_of[seg[panel_order(peers)[k]]]
        copy = pltpu.make_async_copy(down.at[slot], out.at[k, pl.ds(0, rank)], sem.at[k])
        copy.start()
        copies.append(copy)
        hot = jnp.where((row == k) & (col == slot), 1.0, hot)
    picked = jnp.dot(hot.astype(jnp.bfloat16), up[...], preferred_element_type=jnp.float32)
    for k in range(peers):
        rows = [picked[k : k + 1, r * feats : (r + 1) * feats] for r in range(up_rows)]
        out[k, pl.ds(rank, PAD_ROWS), :] = jnp.concatenate(rows, axis=0).astype(jnp.bfloat16)
    for copy in copies:
        copy.wait()


def wanted(peer, step, row_count, chunk):
    shard = (lax.axis_index("tensor") // 2 * 2 + peer % 2) ^ (2 * step)
    return pl.multiple_of(shard * row_count + (peer // 2) * chunk, chunk)


def normed_piece(rows, gain, inv, at):
    return (rows[:, at].astype(jnp.float32) * inv * gain[at].astype(jnp.float32)[None, :]).astype(jnp.bfloat16)


def inv_rms(rows):
    values = rows[...].astype(jnp.float32)
    return lax.rsqrt(jnp.mean(values * values, axis=1, keepdims=True) + EPS)


def norm_send_kernel(steps, row_count, chunk, hidden, gain_hbm, out, held, gain, sem):
    rows = held.shape[0]
    cut = rows // 4
    first = lax.axis_index("pool") * rows
    copies = [pltpu.make_async_copy(gain_hbm, gain, sem.at[4])]
    for i in range(4):
        at = pl.ds(pl.multiple_of(first + i * cut, cut), cut)
        copies.append(pltpu.make_async_copy(hidden.at[at], held.at[pl.ds(i * cut, cut)], sem.at[i]))
    for copy in copies:
        copy.start()
    copies[0].wait()
    for i in range(4):
        copies[1 + i].wait()
        part = held.at[pl.ds(i * cut, cut)]
        inv = inv_rms(part)
        for peer in range(4):
            for step in range(steps):
                at = pl.ds(wanted(peer, step, row_count, chunk), chunk)
                out[peer, pl.ds(i * cut, cut), step * chunk : (step + 1) * chunk] = normed_piece(part, gain, inv, at)


def norm_half_kernel(token, hidden, gain, out):
    half = hidden.shape[1] // 2
    at = pl.ds(pl.multiple_of(lax.axis_index("pool") * half, half), half)
    out[...] = normed_piece(hidden, gain, inv_rms(hidden), at)


def tick_kernel(token, out):
    out[...] = token[...]


def in_order(mine, other, cols):
    me = lax.axis_index("groups") * 2 + lax.axis_index("tensor") % 2
    quarters = [me ^ 3, me ^ 1, me ^ 2, me]
    return jnp.concatenate([half[q, :, cols] for half in (mine, other) for q in quarters], axis=0)


def early_kernel(mine, other, *rest):
    weights, out, last = rest[:-2], rest[-2], rest[-1]
    total = jnp.zeros(out.shape, jnp.float32)
    first = 0
    for w in weights:
        x = in_order(mine, other, slice(first, first + w.shape[0]))
        total += jnp.dot(x, w[...], preferred_element_type=jnp.float32)
        first += w.shape[0]
    out[...] = total
    last[...] = in_order(mine, other, slice(first, mine.shape[2]))


def late_kernel(last, weight, early, out0, out1, out2, own):
    rows = own.shape[0] // 2
    total = early[...] + jnp.dot(last[...], weight[...], preferred_element_type=jnp.float32)
    half = lax.axis_index("pool")
    for part in range(2):
        at = pl.ds(pl.multiple_of((half if part == 0 else 1 - half) * rows, rows), rows)
        for k, out in enumerate((out0, out1, out2, own)):
            first = (4 * part + k) * rows
            out[at, :] = total[first : first + rows].astype(out.dtype)


def rank_kernel(acts, pieces, out):
    rank = out.shape[1]
    feats = pieces.shape[2]
    total = jnp.zeros(out.shape, jnp.float32)
    for k, t in enumerate(panel_order(pieces.shape[0])):
        x = acts[:, t * feats : (t + 1) * feats]
        total += lax.dot_general(x, pieces[k, :rank, :], (((1,), (1,)), ((), ())), preferred_element_type=jnp.float32)
    out[...] = total


def final_kernel(up_rows, own, far0, far1, far2, low_mine, low_other, pieces, out):
    rank = low_mine.shape[1]
    order = panel_order(pieces.shape[0])
    up = [pieces[order.index(t), rank : rank + up_rows, :].astype(jnp.float32) for t in range(len(order))]
    low = (low_mine[...] + low_other[...]).astype(jnp.bfloat16)
    up = jnp.concatenate(up, axis=0).astype(jnp.bfloat16)
    total = jnp.dot(low, up, preferred_element_type=jnp.float32) + own[...]
    for part in (far0, far1, far2):
        total += part[...].astype(jnp.float32)
    out[...] = total.astype(jnp.bfloat16)


def whole(shape):
    return pl.BlockSpec(memory_space=pltpu.VMEM)


def call(kernel, prefetch, args, in_specs, outs, out_specs, grid=(), scratch=(), alias=None, limit=VMEM_LIMIT, name=None, flops=0, nbytes=0):
    return pl.pallas_call(
        kernel,
        grid_spec=pltpu.PrefetchScalarGridSpec(
            num_scalar_prefetch=len(prefetch),
            grid=grid,
            in_specs=in_specs,
            out_specs=out_specs,
            scratch_shapes=scratch,
        ),
        out_shape=outs,
        compiler_params=pltpu.CompilerParams(vmem_limit_bytes=limit),
        input_output_aliases=alias or {},
        cost_estimate=pl.CostEstimate(flops=flops, bytes_accessed=nbytes, transcendentals=0),
        name=name,
    )(*prefetch, *args)


def square_device(hidden, norm_gain, kv_weight, down_panels, up_panels, seg_adapter, slot_of):
    tokens, features = hidden.shape
    groups, peers = lax.axis_size("groups"), lax.axis_size("tensor")
    g = lax.axis_index("groups")
    steps = peers // 2
    row_count, cols = kv_weight.shape
    chunk = row_count // groups
    rows = tokens // 2
    span = steps * chunk
    feats, rank = down_panels.shape[2:]
    bf16, f32 = jnp.bfloat16, jnp.float32
    up_rows = up_panels.shape[2] // feats
    hbm = pl.BlockSpec(memory_space=pltpu.HBM)
    cores = [(0, 1), (1, 0)]

    def to_peer(x, flip_x, flip_g):
        pairs = [(i, i ^ flip_x ^ (flip_g * peers)) for i in range(groups * peers)]
        return lax.ppermute(x, ("groups", "tensor"), pairs)

    own_w = lax.dynamic_slice_in_dim(kv_weight, g * chunk, chunk, 0)


    def along_z(x, step):
        return lax.ppermute(x, "tensor", [(i, i ^ (2 * step)) for i in range(peers)])

    second, first = along_z(own_w, 2), along_z(own_w, 1)
    squares = [[a * peers + z * 2 + x for a in range(groups) for x in range(2)] for z in range(steps)]
    send = call(
        functools.partial(norm_send_kernel, steps, row_count, chunk), [], [hidden, norm_gain], [hbm, hbm],
        jax.ShapeDtypeStruct((4, rows, span), bf16), whole((4, rows, span)),
        scratch=[pltpu.VMEM((rows, features), bf16), pltpu.VMEM((features,), bf16), pltpu.SemaphoreType.DMA((5,))],
        name="norm_send", flops=6 * rows * features, nbytes=4 * rows * features,
    )
    send, later = lax.optimization_barrier((send, slot_of))
    mine = lax.all_to_all(
        send, ("groups", "tensor"), split_axis=0, concat_axis=0, tiled=True, axis_index_groups=squares
    )

    piece_shape = (peers, rank + PAD_ROWS, feats)
    pieces = call(
        gather_kernel, [seg_adapter, later],
        [down_panels[:, 0].transpose(0, 2, 1), up_panels[:, 0]],
        [hbm, whole((up_panels.shape[0], up_panels.shape[2]))],
        jax.ShapeDtypeStruct(piece_shape, bf16), whole(piece_shape),
        scratch=[pltpu.SemaphoreType.DMA((peers,))], name="pick_panels", flops=LONG, nbytes=3 << 20,
    )
    mine, pieces, later, second, first = lax.optimization_barrier((mine, pieces, later, second, first))
    third = along_z(second, 1)
    tick = call(
        tick_kernel, [], [later], [whole(later.shape)], jax.ShapeDtypeStruct(later.shape, jnp.int32),
        whole(later.shape), name="tick", flops=LONG,
    )
    others = [lax.ppermute(mine, "pool", cores)]
    weight = whole((chunk, cols))
    early, x_last = call(
        early_kernel, [], [mine, *others, own_w, first, second],
        [weight] * 5,
        [jax.ShapeDtypeStruct((4 * tokens, cols), f32), jax.ShapeDtypeStruct((4 * tokens, chunk), bf16)],
        [weight] * 2,
        name="early_rows", flops=24 * tokens * chunk * cols, nbytes=4 << 20,
    )
    early, pieces = lax.optimization_barrier((early, pieces))
    tick, early, third = lax.optimization_barrier((tick, early, third))
    late = call(
        late_kernel, [], [x_last, third, early],
        [weight] * 3,
        [jax.ShapeDtypeStruct((tokens, cols), bf16)] * 3 + [jax.ShapeDtypeStruct((tokens, cols), f32)],
        [whole((tokens, cols))] * 4,
        name="late_rows", flops=8 * tokens * chunk * cols, nbytes=4 << 20,
    )
    *late, last = lax.optimization_barrier((*late, tick))
    acts = call(
        norm_half_kernel, [], [last, hidden, norm_gain],
        [pl.BlockSpec(memory_space=pl.ANY), whole((tokens, features)), whole((features,))],
        jax.ShapeDtypeStruct((tokens, features // 2), bf16), whole((tokens, features // 2)),
        name="norm_half", flops=6 * tokens * features, nbytes=4 * tokens * features,
    )
    parts = [to_peer(x, *peer) for x, peer in zip(late[:3], PEERS)]

    pieces = lax.all_to_all(
        pieces, "tensor", split_axis=0, concat_axis=0, tiled=True, axis_index_groups=[panel_order(peers)]
    )
    low_mine = call(
        rank_kernel, [], [acts, pieces], [whole(acts.shape), whole(piece_shape)],
        jax.ShapeDtypeStruct((tokens, rank), f32), whole((tokens, rank)),
        name="low_rank", flops=2 * tokens * rank * features // 2, nbytes=2 << 20,
    )
    low_other = lax.ppermute(low_mine, "pool", cores)
    return call(
        functools.partial(final_kernel, up_rows), [],
        [late[3], *parts, low_mine, low_other, pieces],
        [whole((tokens, cols))] * 4 + [whole((tokens, rank))] * 2 + [whole(piece_shape)],
        jax.ShapeDtypeStruct((tokens, cols), bf16), whole((tokens, cols)),
        name="final", flops=4 * tokens * rank * cols, nbytes=3 << 20,
    )


def gathered_device(hidden, norm_gain, kv_weight, down_panels, up_panels, seg_adapter, slot_of):
    tok_rows = hidden.shape[0]
    half_width = hidden.shape[1] // 2
    peer_count = lax.axis_size("tensor")
    my_half = lax.axis_index("pool")
    seg_local = tok_rows // SEGMENT_TOKENS
    values = hidden.astype(jnp.float32)
    inv_rms = lax.rsqrt(jnp.mean(values * values, axis=1, keepdims=True) + EPS)
    normed = (values * inv_rms * norm_gain.astype(jnp.float32)).astype(jnp.bfloat16)
    weight = lax.all_gather(kv_weight, "tensor", axis=0, tiled=True)
    base = jnp.dot(normed, weight, preferred_element_type=jnp.float32)
    wanted = slot_of[seg_adapter].reshape(peer_count, seg_local).T
    down_store, up_store = down_panels[:, 0], up_panels[:, 0]
    rank_width = down_store.shape[2]
    normed_half = lax.dynamic_slice_in_dim(normed, my_half * half_width, half_width, 1)
    got_down = lax.all_to_all(down_store[wanted], "tensor", split_axis=1, concat_axis=1, tiled=True)
    up_mats = lax.all_to_all(up_store[wanted], "tensor", split_axis=1, concat_axis=1, tiled=True)
    low_rank = jnp.einsum(
        "sti,sir->str",
        normed_half.reshape(seg_local, SEGMENT_TOKENS, half_width),
        got_down.reshape(seg_local, half_width, rank_width),
        preferred_element_type=jnp.float32,
    )
    low_rank = lax.psum(low_rank, "pool").astype(jnp.bfloat16)
    update = jnp.einsum(
        "str,srh->sth",
        low_rank,
        up_mats.reshape(seg_local, rank_width, -1),
        preferred_element_type=jnp.float32,
    )
    return (base + update.reshape(tok_rows, -1)).astype(jnp.bfloat16)


def per_device(hidden, norm_gain, kv_weight, down_panels, up_panels, seg_adapter, slot_of):
    peers, groups = lax.axis_size("tensor"), lax.axis_size("groups")
    feats = down_panels.shape[2]
    fits = (
        hidden.shape[0] == SEGMENT_TOKENS
        and lax.axis_size("pool") == 2
        and peers == 8
        and groups == 2
        and kv_weight.shape[0] % (128 * groups) == 0
        and feats == kv_weight.shape[1]
        and up_panels.shape[2] % (8 * feats) == 0
        and up_panels.shape[2] // feats == PAD_ROWS
    )
    body = square_device if fits else gathered_device
    return body(hidden, norm_gain, kv_weight, down_panels, up_panels, seg_adapter, slot_of)


def solution(mesh):
    placed = (
        P(("groups", "tensor"), None),
        P(),
        P("tensor", "pool"),
        P("groups", "pool", "tensor", None),
        P("groups", "pool", "tensor"),
        P("groups"),
        P("groups"),
    )
    return jax.shard_map(
        per_device,
        mesh=mesh,
        in_specs=placed,
        out_specs=P(("groups", "tensor"), "pool"),
        check_vma=False,
    )
```

```python
import functools

import jax
import jax.numpy as jnp
from jax import lax
from jax.experimental import pallas as pl
from jax.experimental.pallas import tpu as pltpu
from jax.sharding import PartitionSpec as P

SEGMENT_TOKENS = 128
EPS = 1e-05
VMEM_LIMIT = 16 * 1024 * 1024
PAD_ROWS = 8
LONG = 1 << 36
PEERS = ((1, 1), (1, 0), (0, 1))


def panel_order(peers):
    planes = peers // 2
    inner = [*range(planes // 2, -1, -1), *range(planes // 2 + 1, planes)]
    return [2 * z + x for z in inner for x in (1, 0)]


def gather_kernel(seg, slot_of, down, up, out, sem):
    peers = out.shape[0]
    rank, feats = down.shape[1:]
    up_rows = up.shape[1] // feats
    copies = []
    row = lax.broadcasted_iota(jnp.int32, (2 * PAD_ROWS, up.shape[0]), 0)
    col = lax.broadcasted_iota(jnp.int32, (2 * PAD_ROWS, up.shape[0]), 1)
    hot = jnp.zeros((2 * PAD_ROWS, up.shape[0]), jnp.float32)
    for k in range(peers):
        slot = slot_of[seg[panel_order(peers)[k] ^ lax.axis_index("pool")]]
        copy = pltpu.make_async_copy(down.at[slot], out.at[k, pl.ds(0, rank)], sem.at[k])
        copy.start()
        copies.append(copy)
        hot = jnp.where((row == k) & (col == slot), 1.0, hot)
    picked = jnp.dot(hot.astype(jnp.bfloat16), up[...], preferred_element_type=jnp.float32)
    for k in range(peers):
        rows = [picked[k : k + 1, r * feats : (r + 1) * feats] for r in range(up_rows)]
        out[k, pl.ds(rank, PAD_ROWS), :] = jnp.concatenate(rows, axis=0).astype(jnp.bfloat16)
    for copy in copies:
        copy.wait()


def wanted(peer, step, row_count, chunk):
    shard = (lax.axis_index("tensor") // 2 * 2 + peer % 2) ^ (2 * step)
    return pl.multiple_of(shard * row_count + (peer // 2) * chunk, chunk)


def normed_piece(rows, gain, inv, at):
    return (rows[:, at].astype(jnp.float32) * inv * gain[at].astype(jnp.float32)[None, :]).astype(jnp.bfloat16)


def inv_rms(rows):
    values = rows[...].astype(jnp.float32)
    return lax.rsqrt(jnp.mean(values * values, axis=1, keepdims=True) + EPS)


def norm_send_kernel(steps, row_count, chunk, hidden, gain_hbm, out, held, gain, sem):
    rows = held.shape[0]
    cut = rows // 4
    first = lax.axis_index("pool") * rows
    copies = [pltpu.make_async_copy(gain_hbm, gain, sem.at[4])]
    for i in range(4):
        at = pl.ds(pl.multiple_of(first + i * cut, cut), cut)
        copies.append(pltpu.make_async_copy(hidden.at[at], held.at[pl.ds(i * cut, cut)], sem.at[i]))
    for copy in copies:
        copy.start()
    copies[0].wait()
    for i in range(4):
        copies[1 + i].wait()
        part = held.at[pl.ds(i * cut, cut)]
        inv = inv_rms(part)
        for peer in range(4):
            for step in range(steps):
                at = pl.ds(wanted(peer, step, row_count, chunk), chunk)
                out[peer, pl.ds(i * cut, cut), step * chunk : (step + 1) * chunk] = normed_piece(part, gain, inv, at)


def norm_half_kernel(token, hidden, gain, out):
    half = hidden.shape[1] // 2
    at = pl.ds(pl.multiple_of(lax.axis_index("pool") * half, half), half)
    out[...] = normed_piece(hidden, gain, inv_rms(hidden), at)


def tick_kernel(token, out):
    out[...] = token[...]


def in_order(mine, other, cols):
    me = lax.axis_index("groups") * 2 + lax.axis_index("tensor") % 2
    quarters = [me ^ 3, me ^ 1, me ^ 2, me]
    return jnp.concatenate([half[q, :, cols] for half in (mine, other) for q in quarters], axis=0)


def early_kernel(mine, other, *rest):
    weights, out, last = rest[:-2], rest[-2], rest[-1]
    total = jnp.zeros(out.shape, jnp.float32)
    first = 0
    for w in weights:
        x = in_order(mine, other, slice(first, first + w.shape[0]))
        total += jnp.dot(x, w[...], preferred_element_type=jnp.float32)
        first += w.shape[0]
    out[...] = total
    last[...] = in_order(mine, other, slice(first, mine.shape[2]))


def late_kernel(last, weight, early, out0, out1, out2, own):
    rows = own.shape[0] // 2
    total = early[...] + jnp.dot(last[...], weight[...], preferred_element_type=jnp.float32)
    half = lax.axis_index("pool")
    for part in range(2):
        at = pl.ds(pl.multiple_of((half if part == 0 else 1 - half) * rows, rows), rows)
        for k, out in enumerate((out0, out1, out2, own)):
            first = (4 * part + k) * rows
            out[at, :] = total[first : first + rows].astype(out.dtype)


def rank_kernel(acts, pieces, out):
    rank = out.shape[1]
    feats = pieces.shape[2]
    total = jnp.zeros(out.shape, jnp.float32)
    for k, t in enumerate(panel_order(pieces.shape[0])):
        first = (t ^ lax.axis_index("pool")) * feats
        x = acts[:, pl.ds(pl.multiple_of(first, feats), feats)]
        total += lax.dot_general(x, pieces[k, :rank, :], (((1,), (1,)), ((), ())), preferred_element_type=jnp.float32)
    out[...] = total


def final_kernel(up_rows, own, far0, far1, far2, low_mine, low_other, pieces, out, up):
    rank = low_mine.shape[1]
    for k, t in enumerate(panel_order(pieces.shape[0])):
        first = (t ^ lax.axis_index("pool")) * up_rows
        up[pl.ds(pl.multiple_of(first, up_rows), up_rows), :] = pieces[k, rank:, :].astype(jnp.float32)
    low = (low_mine[...] + low_other[...]).astype(jnp.bfloat16)
    total = jnp.dot(low, up[...].astype(jnp.bfloat16), preferred_element_type=jnp.float32) + own[...]
    for part in (far0, far1, far2):
        total += part[...].astype(jnp.float32)
    out[...] = total.astype(jnp.bfloat16)


def whole(shape):
    return pl.BlockSpec(memory_space=pltpu.VMEM)


def call(kernel, prefetch, args, in_specs, outs, out_specs, grid=(), scratch=(), alias=None, limit=VMEM_LIMIT, name=None, flops=0, nbytes=0):
    return pl.pallas_call(
        kernel,
        grid_spec=pltpu.PrefetchScalarGridSpec(
            num_scalar_prefetch=len(prefetch),
            grid=grid,
            in_specs=in_specs,
            out_specs=out_specs,
            scratch_shapes=scratch,
        ),
        out_shape=outs,
        compiler_params=pltpu.CompilerParams(vmem_limit_bytes=limit),
        input_output_aliases=alias or {},
        cost_estimate=pl.CostEstimate(flops=flops, bytes_accessed=nbytes, transcendentals=0),
        name=name,
    )(*prefetch, *args)


def square_device(hidden, norm_gain, kv_weight, down_panels, up_panels, seg_adapter, slot_of):
    tokens, features = hidden.shape
    groups, peers = lax.axis_size("groups"), lax.axis_size("tensor")
    g = lax.axis_index("groups")
    steps = peers // 2
    row_count, cols = kv_weight.shape
    chunk = row_count // groups
    rows = tokens // 2
    span = steps * chunk
    feats, rank = down_panels.shape[2:]
    bf16, f32 = jnp.bfloat16, jnp.float32
    up_rows = up_panels.shape[2] // feats
    hbm = pl.BlockSpec(memory_space=pltpu.HBM)
    cores = [(0, 1), (1, 0)]

    def to_peer(x, flip_x, flip_g):
        pairs = [(i, i ^ flip_x ^ (flip_g * peers)) for i in range(groups * peers)]
        return lax.ppermute(x, ("groups", "tensor"), pairs)

    own_w = lax.dynamic_slice_in_dim(kv_weight, g * chunk, chunk, 0)


    def along_z(x, step):
        return lax.ppermute(x, "tensor", [(i, i ^ (2 * step)) for i in range(peers)])

    second, first = along_z(own_w, 2), along_z(own_w, 1)
    squares = [[a * peers + z * 2 + x for a in range(groups) for x in range(2)] for z in range(steps)]
    send = call(
        functools.partial(norm_send_kernel, steps, row_count, chunk), [], [hidden, norm_gain], [hbm, hbm],
        jax.ShapeDtypeStruct((4, rows, span), bf16), whole((4, rows, span)),
        scratch=[pltpu.VMEM((rows, features), bf16), pltpu.VMEM((features,), bf16), pltpu.SemaphoreType.DMA((5,))],
        name="norm_send", flops=6 * rows * features, nbytes=4 * rows * features,
    )
    send, later = lax.optimization_barrier((send, slot_of))
    mine = lax.all_to_all(
        send, ("groups", "tensor"), split_axis=0, concat_axis=0, tiled=True, axis_index_groups=squares
    )

    piece_shape = (peers, rank + PAD_ROWS, feats)
    pieces = call(
        gather_kernel, [seg_adapter, later],
        [down_panels[:, 0].transpose(0, 2, 1), up_panels[:, 0]],
        [hbm, whole((up_panels.shape[0], up_panels.shape[2]))],
        jax.ShapeDtypeStruct(piece_shape, bf16), whole(piece_shape),
        scratch=[pltpu.SemaphoreType.DMA((peers,))], name="pick_panels", flops=LONG, nbytes=3 << 20,
    )
    mine, pieces, later, second, first = lax.optimization_barrier((mine, pieces, later, second, first))
    third = along_z(second, 1)
    tick = call(
        tick_kernel, [], [later], [whole(later.shape)], jax.ShapeDtypeStruct(later.shape, jnp.int32),
        whole(later.shape), name="tick", flops=LONG,
    )
    others = [lax.ppermute(mine, "pool", cores)]
    weight = whole((chunk, cols))
    early, x_last = call(
        early_kernel, [], [mine, *others, own_w, first, second],
        [weight] * 5,
        [jax.ShapeDtypeStruct((4 * tokens, cols), f32), jax.ShapeDtypeStruct((4 * tokens, chunk), bf16)],
        [weight] * 2,
        name="early_rows", flops=24 * tokens * chunk * cols, nbytes=4 << 20,
    )
    early, pieces = lax.optimization_barrier((early, pieces))
    tick, early, third = lax.optimization_barrier((tick, early, third))
    late = call(
        late_kernel, [], [x_last, third, early],
        [weight] * 3,
        [jax.ShapeDtypeStruct((tokens, cols), bf16)] * 3 + [jax.ShapeDtypeStruct((tokens, cols), f32)],
        [whole((tokens, cols))] * 4,
        name="late_rows", flops=8 * tokens * chunk * cols, nbytes=4 << 20,
    )
    *late, last = lax.optimization_barrier((*late, tick))
    acts = call(
        norm_half_kernel, [], [last, hidden, norm_gain],
        [pl.BlockSpec(memory_space=pl.ANY), whole((tokens, features)), whole((features,))],
        jax.ShapeDtypeStruct((tokens, features // 2), bf16), whole((tokens, features // 2)),
        name="norm_half", flops=6 * tokens * features, nbytes=4 * tokens * features,
    )
    parts = [to_peer(x, *peer) for x, peer in zip(late[:3], PEERS)]

    panel_groups = [
        [(a * peers + (k ^ core)) * 2 + core for k in panel_order(peers)]
        for a in range(groups)
        for core in range(2)
    ]
    pieces = lax.all_to_all(
        pieces, ("groups", "tensor", "pool"), split_axis=0, concat_axis=0, tiled=True, axis_index_groups=panel_groups
    )
    low_mine = call(
        rank_kernel, [], [acts, pieces], [whole(acts.shape), whole(piece_shape)],
        jax.ShapeDtypeStruct((tokens, rank), f32), whole((tokens, rank)),
        name="low_rank", flops=2 * tokens * rank * features // 2, nbytes=2 << 20,
    )
    low_other = lax.ppermute(low_mine, "pool", cores)
    return call(
        functools.partial(final_kernel, up_rows), [],
        [late[3], *parts, low_mine, low_other, pieces],
        [whole((tokens, cols))] * 4 + [whole((tokens, rank))] * 2 + [whole(piece_shape)],
        jax.ShapeDtypeStruct((tokens, cols), bf16), whole((tokens, cols)),
        scratch=[pltpu.VMEM((rank, cols), f32)], name="final", flops=4 * tokens * rank * cols, nbytes=3 << 20,
    )


def gathered_device(hidden, norm_gain, kv_weight, down_panels, up_panels, seg_adapter, slot_of):
    tok_rows = hidden.shape[0]
    half_width = hidden.shape[1] // 2
    peer_count = lax.axis_size("tensor")
    my_half = lax.axis_index("pool")
    seg_local = tok_rows // SEGMENT_TOKENS
    values = hidden.astype(jnp.float32)
    inv_rms = lax.rsqrt(jnp.mean(values * values, axis=1, keepdims=True) + EPS)
    normed = (values * inv_rms * norm_gain.astype(jnp.float32)).astype(jnp.bfloat16)
    weight = lax.all_gather(kv_weight, "tensor", axis=0, tiled=True)
    base = jnp.dot(normed, weight, preferred_element_type=jnp.float32)
    wanted = slot_of[seg_adapter].reshape(peer_count, seg_local).T
    down_store, up_store = down_panels[:, 0], up_panels[:, 0]
    rank_width = down_store.shape[2]
    normed_half = lax.dynamic_slice_in_dim(normed, my_half * half_width, half_width, 1)
    got_down = lax.all_to_all(down_store[wanted], "tensor", split_axis=1, concat_axis=1, tiled=True)
    up_mats = lax.all_to_all(up_store[wanted], "tensor", split_axis=1, concat_axis=1, tiled=True)
    low_rank = jnp.einsum(
        "sti,sir->str",
        normed_half.reshape(seg_local, SEGMENT_TOKENS, half_width),
        got_down.reshape(seg_local, half_width, rank_width),
        preferred_element_type=jnp.float32,
    )
    low_rank = lax.psum(low_rank, "pool").astype(jnp.bfloat16)
    update = jnp.einsum(
        "str,srh->sth",
        low_rank,
        up_mats.reshape(seg_local, rank_width, -1),
        preferred_element_type=jnp.float32,
    )
    return (base + update.reshape(tok_rows, -1)).astype(jnp.bfloat16)


def per_device(hidden, norm_gain, kv_weight, down_panels, up_panels, seg_adapter, slot_of):
    peers, groups = lax.axis_size("tensor"), lax.axis_size("groups")
    feats = down_panels.shape[2]
    fits = (
        hidden.shape[0] == SEGMENT_TOKENS
        and lax.axis_size("pool") == 2
        and peers == 8
        and groups == 2
        and kv_weight.shape[0] % (128 * groups) == 0
        and feats == kv_weight.shape[1]
        and up_panels.shape[2] % (8 * feats) == 0
        and up_panels.shape[2] // feats == PAD_ROWS
    )
    body = square_device if fits else gathered_device
    return body(hidden, norm_gain, kv_weight, down_panels, up_panels, seg_adapter, slot_of)


def solution(mesh):
    placed = (
        P(("groups", "tensor"), None),
        P(),
        P("tensor", "pool"),
        P("groups", "pool", "tensor", None),
        P("groups", "pool", "tensor"),
        P("groups"),
        P("groups"),
    )
    return jax.shard_map(
        per_device,
        mesh=mesh,
        in_specs=placed,
        out_specs=P(("groups", "tensor"), "pool"),
        check_vma=False,
    )
```
